32 devices in a mesh: unit: 16 (over z, y, x), samp: 2 (over core).
Axes of the slice: x: 2, y: 2, z: 4, core: 2. Of those that a mesh axis runs over, the one named last changes fastest.
Arguments:
- abundance: float32 [16384, 4096], P('unit', 'samp'), may hold values from 0.0009 to 27, as said below
- unitig_factor: float32 [16384, 128], P('unit'), may hold values from 0.005 to 1.8, as said below
- sample_factor: float32 [4096, 128], P('samp'), may hold values from 0.02 to 0.2
Outputs:
- unitig_update: float32 [16384, 128], P('unit')
- sample_update: float32 [4096, 128], P('samp')
The draws below stay inside these ranges and needn't reach their ends.
Inputs may be any that keep to these rules, and one draw needn't show every extreme that they name: abundance entries are positive. unitig_factor entries are positive.
All inputs are finite; a program needn't handle non-finite values.
Results may differ from the reference program's by a relative error of at most 0.0001.
Values sent between devices are 32-bit elements; how exact they have to be, the bound alone decides.
A program may use at most 64 MiB of HBM per device.

```python
import math
import jax
import jax.numpy as jnp
from jax import lax

K = 128
ITERS = 2
UNITIGS = 16384
SAMPLES = 4096


def bin_numbers(key):
    return jax.random.randint(jax.random.fold_in(key, 7), (UNITIGS,), 0, K).astype(jnp.int32)


def log_between(key, shape, low, high):
    return jnp.exp(jax.random.uniform(key, shape, jnp.float32, math.log(low), math.log(high)))


def draw_abundance(key, part):
    keys = jax.random.split(jax.random.fold_in(key, 11), 6)
    bins = bin_numbers(key)
    present = jax.random.bernoulli(keys[3], 0.35, (SAMPLES, K))
    row_scale = log_between(keys[0], (UNITIGS, 1), 0.3, 3.0)
    col_scale = log_between(keys[1], (1, SAMPLES), 0.3, 3.0)
    strong = log_between(keys[2], (SAMPLES, K), 0.5, 2.0)
    faint = log_between(keys[4], (SAMPLES, K), 0.02, 0.1)
    noise = log_between(keys[5], (UNITIGS, SAMPLES), 0.5, 1.5)
    profile = jnp.where(present, strong, faint)
    spread = jnp.take(jnp.transpose(profile), bins, axis=0)
    return (row_scale * col_scale * spread * noise).astype(jnp.float32)


def draw_unitig_factor(key, part):
    keys = jax.random.split(jax.random.fold_in(key, 13), 2)
    bins = bin_numbers(key)
    member = bins[:, None] == jnp.arange(K, dtype=jnp.int32)[None, :]
    rising = 1.0 + 2.0 * jnp.arange(UNITIGS, dtype=jnp.float32)[:, None] / max(UNITIGS - 1, 1)
    strong = log_between(keys[0], (UNITIGS, K), 0.2, 0.6)
    faint = log_between(keys[1], (UNITIGS, K), 0.005, 0.03)
    return (jnp.where(member, strong, faint) * rising).astype(jnp.float32)


def shard_levels(rng, dims, cuts, smallest, largest):
    gain, own = 1.0, jax.random.fold_in(rng, 6)
    for axis_at, shards_of in cuts:
        heights = jnp.exp(jax.random.uniform(jax.random.fold_in(own, axis_at), (shards_of,), jnp.float32, smallest / len(cuts), largest / len(cuts)))
        gain = gain * jnp.repeat(heights, dims[axis_at] // shards_of).reshape([-1 if axis == axis_at else 1 for axis in range(len(dims))])
    return gain


def setup_inputs(seed: int = 0) -> dict:
    streams_of = jax.random.split(jax.random.key(seed), 4)
    return {
        "abundance": draw_abundance(jax.random.fold_in(streams_of[3], 71), 0),
        "unitig_factor": draw_unitig_factor(jax.random.fold_in(streams_of[3], 71), 0),
        "sample_factor": jnp.clip(jnp.exp(math.log(0.2) - 2.3025851 * jax.random.uniform(streams_of[2], (SAMPLES, K), jnp.float32) ** shard_levels(streams_of[2], (SAMPLES, K), ((0, 2),), -0.2, 0.2)), 0.02, 0.2),
    }


HI = lax.Precision.HIGHEST


def inner(left, right):
    return lax.dot_general(left, right, (((0,), (0,)), ((), ())), precision=HI, preferred_element_type=jnp.float32)


def reference(abundance, unitig_factor, sample_factor):
    unitig = unitig_factor
    sample = sample_factor
    for sweep in range(ITERS):
        target_h = inner(abundance, unitig)
        gram_unit = inner(unitig, unitig)
        sample = sample * target_h / jnp.dot(sample, gram_unit, precision=HI)
        target_w = jnp.dot(abundance, sample, precision=HI)
        gram_sample = inner(sample, sample)
        unitig = unitig * target_w / jnp.dot(unitig, gram_sample, precision=HI)
    return unitig, sample
```

```python
import functools

import jax
import jax.numpy as jnp
from jax import lax
from jax.experimental import pallas as pl
from jax.experimental.pallas import tpu as pltpu
from jax.sharding import PartitionSpec as P

ITERS = 2
PARTS = 4
HI = lax.Precision.HIGHEST
MESH = pl.DeviceIdType.MESH
BF = jnp.bfloat16


def chip_dims(unit):
    n = 1
    while 2 * n * n * n < unit:
        n += 1
    return (n, n, 2 * n) if 2 * n * n * n == unit else (1, 1, unit)


class Plan:
    def __init__(self, unit, samples, rank):
        self.unit = unit
        self.dims = chip_dims(unit)
        x, y, _ = self.dims
        self.strides = (1, x, x * y)
        self.orders = [(0, 1, 2) if p % 2 == 0 else (1, 0, 2) for p in range(PARTS)]
        self.cols = samples // PARTS
        granule = 8 * unit
        self.used = [self.cols + (rank if p == 0 else 0) for p in range(PARTS)]
        self.rows = [-(-used // granule) * granule for used in self.used]
        self.base = [sum(self.rows[:p]) for p in range(PARTS)]
        self.total = sum(self.rows)
        self.slot, self.sem = {}, {}
        rows = sems = 0
        for p in range(PARTS):
            size = self.rows[p]
            for t in range(3):
                n = self.dims[self.orders[p][t]]
                size //= n
                for k in range(1, n):
                    self.slot[p, t, k] = rows
                    self.sem[p, t, k] = sems
                    rows += size
                    sems += 1
        self.recv_rows, self.sems = max(rows, 8), max(sems, 1)


def split(value):
    high = value.astype(BF)
    return high, (value - high.astype(jnp.float32)).astype(BF)


def dot(left, right):
    return jnp.dot(left, right, preferred_element_type=jnp.float32)


def kernel(
    plan, a_hbm, w_in, h_in, w_ref, h_ref,
    a_f32, a_high, a_low, wt, acc, gat, rsr, q_own, q_peer, f_sum,
    load_sem, rs_send, rs_recv, ag_send, ag_recv, q_send, q_recv,
):
    units, rank = w_in.shape
    cols = plan.cols
    me = lax.axis_index("unit")
    core = lax.axis_index("samp")
    place = [lax.rem(me // plan.strides[d], plan.dims[d]) for d in range(3)]
    block = 256

    loads = [
        pltpu.make_async_copy(
            a_hbm.at[:, pl.ds(p * cols, cols)], a_f32.at[p], load_sem.at[p]
        )
        for p in range(PARTS)
    ]
    for load in loads:
        load.start()

    def peer_of(d, k):
        other = lax.rem(place[d] + k, plan.dims[d])
        return other, me + (other - place[d]) * plan.strides[d]

    barrier = pltpu.get_barrier_semaphore()
    greeted = 1
    pl.semaphore_signal(barrier, inc=1, device_id={"samp": 1 - core}, device_id_type=MESH)
    for d in range(3):
        for k in range(1, plan.dims[d]):
            pl.semaphore_signal(
                barrier, inc=1, device_id={"unit": peer_of(d, k)[1]}, device_id_type=MESH
            )
            greeted += 1
    pl.semaphore_wait(barrier, greeted)

    offs, sizes = [], []
    for p in range(PARTS):
        off, size = plan.base[p], plan.rows[p]
        offs.append([off])
        sizes.append([size])
        for t in range(3):
            d = plan.orders[p][t]
            size //= plan.dims[d]
            off = off + place[d] * size
            offs[p].append(off)
            sizes[p].append(size)

    def rows_at(off, size):
        return pl.ds(off if isinstance(off, int) else pl.multiple_of(off, 8), size)

    def rs_copies(it, p, t):
        d, size = plan.orders[p][t], sizes[p][t + 1]
        copies = []
        for k in range(1, plan.dims[d]):
            other, device = peer_of(d, k)
            sem = plan.sem[p, t, k]
            copies.append(pltpu.make_async_remote_copy(
                src_ref=acc.at[it, rows_at(offs[p][t] + other * size, size)],
                dst_ref=rsr.at[it, pl.ds(plan.slot[p, t, k], size)],
                send_sem=rs_send.at[it, sem],
                recv_sem=rs_recv.at[it, sem],
                device_id={"unit": device},
                device_id_type=MESH,
            ))
        return copies

    def ag_copies(it, p, t):
        d, size = plan.orders[p][t], sizes[p][t + 1]
        copies = []
        for k in range(1, plan.dims[d]):
            _, device = peer_of(d, k)
            sem = plan.sem[p, t, k]
            here = gat.at[it, rows_at(offs[p][t + 1], size)]
            copies.append(pltpu.make_async_remote_copy(
                src_ref=here,
                dst_ref=here,
                send_sem=ag_send.at[it, sem],
                recv_sem=ag_recv.at[it, sem],
                device_id={"unit": device},
                device_id_type=MESH,
            ))
        return copies

    def q_copy(it, b, start, size):
        return pltpu.make_async_remote_copy(
            src_ref=q_own.at[it, pl.ds(start, size)],
            dst_ref=q_peer.at[it, pl.ds(start, size)],
            send_sem=q_send.at[it, b],
            recv_sem=q_recv.at[it, b],
            device_id={"samp": 1 - core},
            device_id_type=MESH,
        )

    def start_all(copies):
        for copy in copies:
            copy.start()

    w_ref[...] = w_in[...]
    h_ref[...] = h_in[...]
    turned = w_in[...].T
    wt[:rank], wt[rank:] = split(turned)

    for it in range(ITERS):
        sent = []
        for p in range(PARTS):
            if p == 0:
                acc[it, pl.ds(plan.base[0] + cols, rank)] = jnp.dot(
                    w_ref[...].T, w_ref[...], precision=HI, preferred_element_type=jnp.float32
                )
            if plan.rows[p] > plan.used[p]:
                spare = plan.rows[p] - plan.used[p]
                acc[it, pl.ds(plan.base[p] + plan.used[p], spare)] = jnp.zeros(
                    (spare, rank), jnp.float32
                )
            if it == 0:
                loads[p].wait()
                a_high[p], a_low[p] = split(a_f32[p])
            both = dot(wt[...], a_high[p])
            product = both[:rank] + (both[rank:] + dot(wt[:rank], a_low[p]))
            acc[it, pl.ds(plan.base[p], cols)] = product.T
            copies = rs_copies(it, p, 0)
            start_all(copies)
            sent.append(copies)

        for t in range(3):
            for p in range(PARTS):
                size = sizes[p][t + 1]
                mine = rows_at(offs[p][t + 1], size)
                n = plan.dims[plan.orders[p][t]]
                for copy in sent[p]:
                    copy.wait()
                value = acc[it, mine]
                for k in range(1, n):
                    value = value + rsr[it, pl.ds(plan.slot[p, t, k], size)]
                if t < 2:
                    acc[it, mine] = value
                    sent[p] = rs_copies(it, p, t + 1)
                else:
                    gat[it, mine] = value
                    sent[p] = ag_copies(it, p, 2)
                start_all(sent[p])

        for t in (2, 1, 0):
            for p in range(PARTS):
                for copy in sent[p]:
                    copy.wait()
                if t > 0:
                    sent[p] = ag_copies(it, p, t - 1)
                    start_all(sent[p])
                    continue
                here = pl.ds(p * cols, cols)
                old = h_ref[here]
                gram = gat[it, pl.ds(plan.base[0] + cols, rank)]
                new = old * gat[it, pl.ds(plan.base[p], cols)] / jnp.dot(
                    old, gram, precision=HI, preferred_element_type=jnp.float32
                )
                h_ref[here] = new
                part_f = jnp.dot(
                    new.T, new, precision=HI, preferred_element_type=jnp.float32
                )
                tail = pl.ds(units, rank)
                q_own[it, tail] = part_f if p == 0 else q_own[it, tail] + part_f
                crossing = []
                if p == PARTS - 1:
                    crossing.append(q_copy(it, 0, units, rank))
                    crossing[0].start()
                high, low = split(new)
                pair = jnp.concatenate([high, low], axis=1)
                for b in range(units // block):
                    rows = pl.ds(b * block, block)
                    both = dot(a_high[p, rows], pair)
                    value = both[:, :rank] + (both[:, rank:] + dot(a_low[p, rows], high))
                    q_own[it, rows] = value if p == 0 else q_own[it, rows] + value
                    if p == PARTS - 1:
                        crossing.append(q_copy(it, b + 1, b * block, block))
                        crossing[-1].start()

        crossing[0].wait()
        f_sum[...] = q_own[it, pl.ds(units, rank)] + q_peer[it, pl.ds(units, rank)]
        for b in range(units // block):
            rows = pl.ds(b * block, block)
            crossing[b + 1].wait()
            old = w_ref[rows]
            new = old * (q_own[it, rows] + q_peer[it, rows]) / jnp.dot(
                old, f_sum[...], precision=HI, preferred_element_type=jnp.float32
            )
            w_ref[rows] = new
            if it < ITERS - 1:
                wt[:rank, rows], wt[rank:, rows] = split(new.T)


def shards(unit, abundance, unitig_factor, sample_factor):
    units, samples = abundance.shape
    rank = unitig_factor.shape[1]
    plan = Plan(unit, samples, rank)
    cols = plan.cols
    f32 = jnp.float32
    vmem = pl.BlockSpec(memory_space=pltpu.VMEM)
    blocks = units // 256 + 1
    flops = 4 * 3 * 2 * units * samples * rank
    return pl.pallas_call(
        functools.partial(kernel, plan),
        out_shape=(
            jax.ShapeDtypeStruct((units, rank), f32),
            jax.ShapeDtypeStruct((samples, rank), f32),
        ),
        in_specs=[pl.BlockSpec(memory_space=pl.ANY), vmem, vmem],
        out_specs=(vmem, vmem),
        scratch_shapes=[
            pltpu.VMEM((PARTS, units, cols), f32),
            pltpu.VMEM((PARTS, units, cols), BF),
            pltpu.VMEM((PARTS, units, cols), BF),
            pltpu.VMEM((2 * rank, units), BF),
            pltpu.VMEM((ITERS, plan.total, rank), f32),
            pltpu.VMEM((ITERS, plan.total, rank), f32),
            pltpu.VMEM((ITERS, plan.recv_rows, rank), f32),
            pltpu.VMEM((ITERS, units + rank, rank), f32),
            pltpu.VMEM((ITERS, units + rank, rank), f32),
            pltpu.VMEM((rank, rank), f32),
            pltpu.SemaphoreType.DMA((PARTS,)),
            pltpu.SemaphoreType.DMA((ITERS, plan.sems)),
            pltpu.SemaphoreType.DMA((ITERS, plan.sems)),
            pltpu.SemaphoreType.DMA((ITERS, plan.sems)),
            pltpu.SemaphoreType.DMA((ITERS, plan.sems)),
            pltpu.SemaphoreType.DMA((ITERS, blocks)),
            pltpu.SemaphoreType.DMA((ITERS, blocks)),
        ],
        compiler_params=pltpu.CompilerParams(
            collective_id=0, has_side_effects=True, vmem_limit_bytes=56 * 2**20
        ),
        cost_estimate=pl.CostEstimate(
            flops=flops, bytes_accessed=4 * units * samples, transcendentals=0
        ),
    )(abundance, unitig_factor, sample_factor)


def solution(mesh):
    return jax.shard_map(
        functools.partial(shards, mesh.shape["unit"]),
        mesh=mesh,
        in_specs=(P("unit", "samp"), P("unit", None), P("samp", None)),
        out_specs=(P("unit", None), P("samp", None)),
        check_vma=False,
    )
```

```python
import functools

import jax
import jax.numpy as jnp
from jax import lax
from jax.experimental import pallas as pl
from jax.experimental.pallas import tpu as pltpu
from jax.sharding import PartitionSpec as P

ITERS = 2
PARTS = 4
MESH = pl.DeviceIdType.MESH
BF = jnp.bfloat16


def chip_dims(unit):
    n = 1
    while 2 * n * n * n < unit:
        n += 1
    return (n, n, 2 * n) if 2 * n * n * n == unit else (1, 1, unit)


class Plan:
    def __init__(self, unit, samples, rank):
        self.unit = unit
        self.dims = chip_dims(unit)
        x, y, _ = self.dims
        self.strides = (1, x, x * y)
        self.orders = [(0, 1, 2) if p % 2 == 0 else (1, 0, 2) for p in range(PARTS)]
        self.cols = samples // PARTS
        granule = 8 * unit
        self.used = [self.cols + (rank if p == 0 else 0) for p in range(PARTS)]
        self.rows = [-(-used // granule) * granule for used in self.used]
        self.base = [sum(self.rows[:p]) for p in range(PARTS)]
        self.total = sum(self.rows)
        self.slot, self.sem = {}, {}
        rows = sems = 0
        for p in range(PARTS):
            size = self.rows[p]
            for t in range(3):
                n = self.dims[self.orders[p][t]]
                size //= n
                for k in range(1, n):
                    self.slot[p, t, k] = rows
                    self.sem[p, t, k] = sems
                    rows += size
                    sems += 1
        self.recv_rows, self.sems = max(rows, 8), max(sems, 1)


def split(value):
    high = value.astype(BF)
    return high, (value - high.astype(jnp.float32)).astype(BF)


def dot(left, right):
    return jnp.dot(left, right, preferred_element_type=jnp.float32)


def pack(square):
    high, low = split(square)
    return jnp.concatenate(
        [
            jnp.concatenate([high, low], axis=1),
            jnp.concatenate([high, jnp.zeros_like(high)], axis=1),
        ],
        axis=0,
    )


def dot_packed(left, packed):
    rank = left.shape[1]
    both = dot(jnp.concatenate(split(left), axis=1), packed)
    return both[:, :rank] + both[:, rank:]


def gram_of(turned, pair):
    rank = turned.shape[0] // 2
    four = dot(turned, pair)
    return four[:rank, :rank] + (
        four[rank:, :rank] + four[:rank, rank:] + four[rank:, rank:]
    )


EVENTS = (
    (0, 0), (1, 0), (0, 1), (1, 1), (2, 0), (3, 0), (0, 2), (1, 2), (2, 1), (3, 1),
    (0, 3), (1, 3), (2, 2), (3, 2), (0, 4), (1, 4), (0, 5), (2, 3), (3, 3), (1, 5),
    (2, 4), (3, 4), (2, 5), (3, 5),
)


def kernel(
    plan, a_hbm, w_in, h_in, w_ref, h_out,
    a_f32, a_high, a_low, wt, acc, gat, rsr, q_own, q_peer, g_pack, f_pack, h_ref,
    load_sem, h_sem, rs_send, rs_recv, ag_send, ag_recv, q_send, q_recv,
):
    units, rank = w_in.shape
    cols = plan.cols
    me = lax.axis_index("unit")
    core = lax.axis_index("samp")
    place = [lax.rem(me // plan.strides[d], plan.dims[d]) for d in range(3)]
    block = 256

    loads = [
        pltpu.make_async_copy(
            a_hbm.at[:, pl.ds(p * cols, cols)], a_f32.at[p], load_sem.at[p]
        )
        for p in range(PARTS)
    ]
    for load in loads:
        load.start()
    h_load = pltpu.make_async_copy(h_in, h_ref, h_sem)
    h_load.start()

    def peer_of(d, k):
        other = lax.rem(place[d] + k, plan.dims[d])
        return other, me + (other - place[d]) * plan.strides[d]

    barrier = pltpu.get_barrier_semaphore()
    greeted = 1
    pl.semaphore_signal(barrier, inc=1, device_id={"samp": 1 - core}, device_id_type=MESH)
    for d in range(3):
        for k in range(1, plan.dims[d]):
            pl.semaphore_signal(
                barrier, inc=1, device_id={"unit": peer_of(d, k)[1]}, device_id_type=MESH
            )
            greeted += 1
    offs, sizes = [], []
    for p in range(PARTS):
        off, size = plan.base[p], plan.rows[p]
        offs.append([off])
        sizes.append([size])
        for t in range(3):
            d = plan.orders[p][t]
            size //= plan.dims[d]
            off = off + place[d] * size
            offs[p].append(off)
            sizes[p].append(size)

    def rows_at(off, size):
        return pl.ds(off if isinstance(off, int) else pl.multiple_of(off, 8), size)

    def rs_copies(it, p, t):
        d, size = plan.orders[p][t], sizes[p][t + 1]
        copies = []
        for k in range(1, plan.dims[d]):
            other, device = peer_of(d, k)
            sem = plan.sem[p, t, k]
            copies.append(pltpu.make_async_remote_copy(
                src_ref=acc.at[it, rows_at(offs[p][t] + other * size, size)],
                dst_ref=rsr.at[it, pl.ds(plan.slot[p, t, k], size)],
                send_sem=rs_send.at[it, sem],
                recv_sem=rs_recv.at[it, sem],
                device_id={"unit": device},
                device_id_type=MESH,
            ))
        return copies

    def ag_copies(it, p, t):
        d, size = plan.orders[p][t], sizes[p][t + 1]
        copies = []
        for k in range(1, plan.dims[d]):
            _, device = peer_of(d, k)
            sem = plan.sem[p, t, k]
            here = gat.at[it, rows_at(offs[p][t + 1], size)]
            copies.append(pltpu.make_async_remote_copy(
                src_ref=here,
                dst_ref=here,
                send_sem=ag_send.at[it, sem],
                recv_sem=ag_recv.at[it, sem],
                device_id={"unit": device},
                device_id_type=MESH,
            ))
        return copies

    def q_copy(it, b, start, size):
        return pltpu.make_async_remote_copy(
            src_ref=q_own.at[it, pl.ds(start, size)],
            dst_ref=q_peer.at[it, pl.ds(start, size)],
            send_sem=q_send.at[it, b],
            recv_sem=q_recv.at[it, b],
            device_id={"samp": 1 - core},
            device_id_type=MESH,
        )

    def start_all(copies):
        for copy in copies:
            copy.start()

    def products(it, p, sent):
        if p == 0:
            acc[it, pl.ds(plan.base[0] + cols, rank)] = gram_of(
                wt[...], jnp.concatenate(split(w_ref[...]), axis=1)
            )
        if plan.rows[p] > plan.used[p]:
            spare = plan.rows[p] - plan.used[p]
            acc[it, pl.ds(plan.base[p] + plan.used[p], spare)] = jnp.zeros(
                (spare, rank), jnp.float32
            )
        if it == 0:
            loads[p].wait()
            a_high[p], a_low[p] = split(a_f32[p])
        both = dot(wt[...], a_high[p])
        product = both[:rank] + (both[rank:] + dot(wt[:rank], a_low[p]))
        acc[it, pl.ds(plan.base[p], cols)] = product.T
        if it == 0 and p == 0:
            pl.semaphore_wait(barrier, greeted)
        sent[p] = rs_copies(it, p, 0)
        start_all(sent[p])

    def advance(it, p, stage, sent):
        for copy in sent[p]:
            copy.wait()
        if stage < 3:
            size = sizes[p][stage + 1]
            mine = rows_at(offs[p][stage + 1], size)
            value = acc[it, mine]
            for k in range(1, plan.dims[plan.orders[p][stage]]):
                value = value + rsr[it, pl.ds(plan.slot[p, stage, k], size)]
            if stage < 2:
                acc[it, mine] = value
                sent[p] = rs_copies(it, p, stage + 1)
            else:
                gat[it, mine] = value
                sent[p] = ag_copies(it, p, 2)
            start_all(sent[p])
        elif stage < 5:
            sent[p] = ag_copies(it, p, 4 - stage)
            start_all(sent[p])

    def update_sample(it, p, h_store):
        if p == 0:
            g_pack[...] = pack(gat[it, pl.ds(plan.base[0] + cols, rank)])
        here = pl.ds(p * cols, cols)
        old = h_ref[here]
        new = old * gat[it, pl.ds(plan.base[p], cols)] / dot_packed(old, g_pack[...])
        h_ref[here] = new
        if it == ITERS - 1:
            h_store[p].start()
        pair = jnp.concatenate(split(new), axis=1)
        turned = jnp.concatenate(split(new.T), axis=0)
        part_f = gram_of(turned, pair)
        tail = pl.ds(units, rank)
        q_own[it, tail] = part_f if p == 0 else q_own[it, tail] + part_f
        crossing = []
        if p == PARTS - 1:
            crossing.append(q_copy(it, 0, units, rank))
            crossing[0].start()
        for b in range(units // block):
            rows = pl.ds(b * block, block)
            both = dot(a_high[p, rows], pair)
            value = both[:, :rank] + (both[:, rank:] + dot(a_low[p, rows], pair[:, :rank]))
            q_own[it, rows] = value if p == 0 else q_own[it, rows] + value
            if p == PARTS - 1:
                crossing.append(q_copy(it, b + 1, b * block, block))
                crossing[-1].start()
        return crossing

    w_ref[...] = w_in[...]
    turned = w_in[...].T
    wt[:rank], wt[rank:] = split(turned)
    h_store = [
        pltpu.make_async_copy(
            h_ref.at[pl.ds(p * cols, cols)], h_out.at[pl.ds(p * cols, cols)], load_sem.at[p]
        )
        for p in range(PARTS)
    ]

    for it in range(ITERS):
        sent = {}
        for p in range(PARTS):
            products(it, p, sent)
        if it == 0:
            h_load.wait()
        crossing = []
        for p, stage in EVENTS:
            advance(it, p, stage, sent)
            if stage == 5:
                crossing = update_sample(it, p, h_store)

        crossing[0].wait()
        f_pack[...] = pack(q_own[it, pl.ds(units, rank)] + q_peer[it, pl.ds(units, rank)])
        for b in range(units // block):
            rows = pl.ds(b * block, block)
            crossing[b + 1].wait()
            old = w_ref[rows]
            new = old * (q_own[it, rows] + q_peer[it, rows]) / dot_packed(old, f_pack[...])
            w_ref[rows] = new
            if it < ITERS - 1:
                wt[:rank, rows], wt[rank:, rows] = split(new.T)
    for store in h_store:
        store.wait()


def carry(w_ref, h_ref, w_out, h_out, sems):
    copies = [
        pltpu.make_async_copy(w_ref, w_out, sems.at[0]),
        pltpu.make_async_copy(h_ref, h_out, sems.at[1]),
    ]
    for copy in copies:
        copy.start()
    for copy in copies:
        copy.wait()


def shards(unit, abundance, unitig_factor, sample_factor):
    units, samples = abundance.shape
    rank = unitig_factor.shape[1]
    plan = Plan(unit, samples, rank)
    cols = plan.cols
    f32 = jnp.float32
    vmem = pl.BlockSpec(memory_space=pltpu.VMEM)
    blocks = units // 256 + 1
    flops = 4 * 3 * 2 * units * samples * rank
    hbm = pl.BlockSpec(memory_space=pl.ANY)
    results = (
        jax.ShapeDtypeStruct((units, rank), f32),
        jax.ShapeDtypeStruct((samples, rank), f32),
    )
    w_new, h_new = pl.pallas_call(
        functools.partial(kernel, plan),
        out_shape=results,
        in_specs=[hbm, vmem, hbm],
        out_specs=(vmem, hbm),
        scratch_shapes=[
            pltpu.VMEM((PARTS, units, cols), f32),
            pltpu.VMEM((PARTS, units, cols), BF),
            pltpu.VMEM((PARTS, units, cols), BF),
            pltpu.VMEM((2 * rank, units), BF),
            pltpu.VMEM((ITERS, plan.total, rank), f32),
            pltpu.VMEM((ITERS, plan.total, rank), f32),
            pltpu.VMEM((ITERS, plan.recv_rows, rank), f32),
            pltpu.VMEM((ITERS, units + rank, rank), f32),
            pltpu.VMEM((ITERS, units + rank, rank), f32),
            pltpu.VMEM((2 * rank, 2 * rank), BF),
            pltpu.VMEM((2 * rank, 2 * rank), BF),
            pltpu.VMEM((samples, rank), f32),
            pltpu.SemaphoreType.DMA((PARTS,)),
            pltpu.SemaphoreType.DMA,
            pltpu.SemaphoreType.DMA((ITERS, plan.sems)),
            pltpu.SemaphoreType.DMA((ITERS, plan.sems)),
            pltpu.SemaphoreType.DMA((ITERS, plan.sems)),
            pltpu.SemaphoreType.DMA((ITERS, plan.sems)),
            pltpu.SemaphoreType.DMA((ITERS, blocks)),
            pltpu.SemaphoreType.DMA((ITERS, blocks)),
        ],
        compiler_params=pltpu.CompilerParams(
            collective_id=0, has_side_effects=True, vmem_limit_bytes=56 * 2**20
        ),
        cost_estimate=pl.CostEstimate(
            flops=flops, bytes_accessed=4 * units * samples, transcendentals=0
        ),
    )(abundance, unitig_factor, sample_factor)
    return pl.pallas_call(
        carry,
        out_shape=results,
        in_specs=[hbm, hbm],
        out_specs=(hbm, hbm),
        scratch_shapes=[pltpu.SemaphoreType.DMA((2,))],
    )(w_new, h_new)


def solution(mesh):
    return jax.shard_map(
        functools.partial(shards, mesh.shape["unit"]),
        mesh=mesh,
        in_specs=(P("unit", "samp"), P("unit", None), P("samp", None)),
        out_specs=(P("unit", None), P("samp", None)),
        check_vma=False,
    )
```

```python
import functools

import jax
import jax.numpy as jnp
from jax import lax
from jax.experimental import pallas as pl
from jax.experimental.pallas import tpu as pltpu
from jax.sharding import PartitionSpec as P

ITERS = 2
PARTS = 4
MESH = pl.DeviceIdType.MESH
BF = jnp.bfloat16


def chip_dims(unit):
    n = 1
    while 2 * n * n * n < unit:
        n += 1
    return (n, n, 2 * n) if 2 * n * n * n == unit else (1, 1, unit)


class Plan:
    def __init__(self, unit, samples, rank):
        self.unit = unit
        self.dims = chip_dims(unit)
        x, y, _ = self.dims
        self.strides = (1, x, x * y)
        self.orders = [(0, 1, 2) if p % 2 == 0 else (1, 0, 2) for p in range(PARTS)]
        self.cols = samples // PARTS
        granule = 8 * unit
        self.used = [self.cols + (rank if p == 0 else 0) for p in range(PARTS)]
        self.rows = [-(-used // granule) * granule for used in self.used]
        self.base = [sum(self.rows[:p]) for p in range(PARTS)]
        self.total = sum(self.rows)
        self.slot, self.sem = {}, {}
        rows = sems = 0
        for p in range(PARTS):
            size = self.rows[p]
            for t in range(3):
                n = self.dims[self.orders[p][t]]
                size //= n
                for k in range(1, n):
                    self.slot[p, t, k] = rows
                    self.sem[p, t, k] = sems
                    rows += size
                    sems += 1
        self.recv_rows, self.sems = max(rows, 8), max(sems, 1)


def split(value):
    high = value.astype(BF)
    return high, (value - high.astype(jnp.float32)).astype(BF)


def dot(left, right):
    return jnp.dot(left, right, preferred_element_type=jnp.float32)


def pack(square):
    high, low = split(square)
    return jnp.concatenate(
        [
            jnp.concatenate([high, low], axis=1),
            jnp.concatenate([high, jnp.zeros_like(high)], axis=1),
        ],
        axis=0,
    )


def dot_packed(left, packed):
    rank = left.shape[1]
    both = dot(jnp.concatenate(split(left), axis=1), packed)
    return both[:, :rank] + both[:, rank:]


def gram_of(turned, pair):
    rank = turned.shape[0] // 2
    four = dot(turned, pair)
    return four[:rank, :rank] + (
        four[rank:, :rank] + four[:rank, rank:] + four[rank:, rank:]
    )


EVENTS = (
    (0, 0), (1, 0), (0, 1), (1, 1), (2, 0), (3, 0), (0, 2), (1, 2), (2, 1), (3, 1),
    (0, 3), (1, 3), (2, 2), (3, 2), (0, 4), (1, 4), (0, 5), (2, 3), (3, 3), (1, 5),
    (2, 4), (3, 4), (2, 5), (3, 5),
)


def kernel(
    plan, a_hbm, w_in, h_in, w_ref, h_out,
    a_f32, a_high, a_low, wt, acc, gat, rsr, q_own, q_peer, g_pack, f_pack, h_ref, pair_ref,
    load_sem, h_sem, rs_send, rs_recv, ag_send, ag_recv, q_send, q_recv,
):
    units, rank = w_in.shape
    cols = plan.cols
    me = lax.axis_index("unit")
    core = lax.axis_index("samp")
    place = [lax.rem(me // plan.strides[d], plan.dims[d]) for d in range(3)]
    block = 256

    loads = [
        pltpu.make_async_copy(
            a_hbm.at[:, pl.ds(p * cols, cols)], a_f32.at[p], load_sem.at[p]
        )
        for p in range(PARTS)
    ]
    for load in loads:
        load.start()
    h_load = pltpu.make_async_copy(h_in, h_ref, h_sem)
    h_load.start()

    def peer_of(d, k):
        other = lax.rem(place[d] + k, plan.dims[d])
        return other, me + (other - place[d]) * plan.strides[d]

    barrier = pltpu.get_barrier_semaphore()
    greeted = 1
    pl.semaphore_signal(barrier, inc=1, device_id={"samp": 1 - core}, device_id_type=MESH)
    for d in range(3):
        for k in range(1, plan.dims[d]):
            pl.semaphore_signal(
                barrier, inc=1, device_id={"unit": peer_of(d, k)[1]}, device_id_type=MESH
            )
            greeted += 1
    offs, sizes = [], []
    for p in range(PARTS):
        off, size = plan.base[p], plan.rows[p]
        offs.append([off])
        sizes.append([size])
        for t in range(3):
            d = plan.orders[p][t]
            size //= plan.dims[d]
            off = off + place[d] * size
            offs[p].append(off)
            sizes[p].append(size)

    def rows_at(off, size):
        return pl.ds(off if isinstance(off, int) else pl.multiple_of(off, 8), size)

    def rs_copies(it, p, t):
        d, size = plan.orders[p][t], sizes[p][t + 1]
        copies = []
        for k in range(1, plan.dims[d]):
            other, device = peer_of(d, k)
            sem = plan.sem[p, t, k]
            copies.append(pltpu.make_async_remote_copy(
                src_ref=acc.at[it, rows_at(offs[p][t] + other * size, size)],
                dst_ref=rsr.at[it, pl.ds(plan.slot[p, t, k], size)],
                send_sem=rs_send.at[it, sem],
                recv_sem=rs_recv.at[it, sem],
                device_id={"unit": device},
                device_id_type=MESH,
            ))
        return copies

    def ag_copies(it, p, t):
        d, size = plan.orders[p][t], sizes[p][t + 1]
        copies = []
        for k in range(1, plan.dims[d]):
            _, device = peer_of(d, k)
            sem = plan.sem[p, t, k]
            here = gat.at[it, rows_at(offs[p][t + 1], size)]
            copies.append(pltpu.make_async_remote_copy(
                src_ref=here,
                dst_ref=here,
                send_sem=ag_send.at[it, sem],
                recv_sem=ag_recv.at[it, sem],
                device_id={"unit": device},
                device_id_type=MESH,
            ))
        return copies

    def q_copy(it, b, start, size):
        return pltpu.make_async_remote_copy(
            src_ref=q_own.at[it, pl.ds(start, size)],
            dst_ref=q_peer.at[it, pl.ds(start, size)],
            send_sem=q_send.at[it, b],
            recv_sem=q_recv.at[it, b],
            device_id={"samp": 1 - core},
            device_id_type=MESH,
        )

    def start_all(copies):
        for copy in copies:
            copy.start()

    def products(it, p, sent):
        if p == 0:
            acc[it, pl.ds(plan.base[0] + cols, rank)] = gram_of(
                wt[...], jnp.concatenate(split(w_ref[...]), axis=1)
            )
        if plan.rows[p] > plan.used[p]:
            spare = plan.rows[p] - plan.used[p]
            acc[it, pl.ds(plan.base[p] + plan.used[p], spare)] = jnp.zeros(
                (spare, rank), jnp.float32
            )

        @pl.when(it == 0)
        def _():
            loads[p].wait()

            @pl.loop(0, units // block)
            def _(b):
                rows = pl.ds(pl.multiple_of(b * block, block), block)
                a_high[p, rows], a_low[p, rows] = split(a_f32[p, rows])

        both = dot(wt[...], a_high[p])
        product = both[:rank] + (both[rank:] + dot(wt[:rank], a_low[p]))
        acc[it, pl.ds(plan.base[p], cols)] = product.T
        sent[p] = rs_copies(it, p, 0)
        start_all(sent[p])

    def advance(it, p, stage, sent):
        for copy in sent[p]:
            copy.wait()
        if stage < 3:
            size = sizes[p][stage + 1]
            mine = rows_at(offs[p][stage + 1], size)
            value = acc[it, mine]
            for k in range(1, plan.dims[plan.orders[p][stage]]):
                value = value + rsr[it, pl.ds(plan.slot[p, stage, k], size)]
            if stage < 2:
                acc[it, mine] = value
                sent[p] = rs_copies(it, p, stage + 1)
            else:
                gat[it, mine] = value
                sent[p] = ag_copies(it, p, 2)
            start_all(sent[p])
        elif stage < 5:
            sent[p] = ag_copies(it, p, 4 - stage)
            start_all(sent[p])

    def update_sample(it, p, h_store):
        if p == 0:
            g_pack[...] = pack(gat[it, pl.ds(plan.base[0] + cols, rank)])
        here = pl.ds(p * cols, cols)
        old = h_ref[here]
        new = old * gat[it, pl.ds(plan.base[p], cols)] / dot_packed(old, g_pack[...])
        h_ref[here] = new

        @pl.when(it == ITERS - 1)
        def _():
            h_store[p].start()

        pair = jnp.concatenate(split(new), axis=1)
        turned = jnp.concatenate(split(new.T), axis=0)
        part_f = gram_of(turned, pair)
        tail = pl.ds(units, rank)
        q_own[it, tail] = part_f if p == 0 else q_own[it, tail] + part_f
        if p == PARTS - 1:
            q_copy(it, units // block, units, rank).start()
        pair_ref[...] = pair

        @pl.loop(0, units // block)
        def _(b):
            first = pl.multiple_of(b * block, block)
            rows = pl.ds(first, block)
            both = dot(a_high[p, rows], pair_ref[...])
            value = both[:, :rank] + (both[:, rank:] + dot(a_low[p, rows], pair_ref[:, :rank]))
            q_own[it, rows] = value if p == 0 else q_own[it, rows] + value
            if p == PARTS - 1:
                q_copy(it, b, first, block).start()

    w_ref[...] = w_in[...]
    turned = w_in[...].T
    wt[:rank], wt[rank:] = split(turned)
    h_store = [
        pltpu.make_async_copy(
            h_ref.at[pl.ds(p * cols, cols)], h_out.at[pl.ds(p * cols, cols)], load_sem.at[p]
        )
        for p in range(PARTS)
    ]

    h_load.wait()
    pl.semaphore_wait(barrier, greeted)

    @pl.loop(0, ITERS)
    def _(it):
        sent = {}
        for p in range(PARTS):
            products(it, p, sent)
        for p, stage in EVENTS:
            advance(it, p, stage, sent)
            if stage == 5:
                update_sample(it, p, h_store)

        q_copy(it, units // block, units, rank).wait()
        f_pack[...] = pack(q_own[it, pl.ds(units, rank)] + q_peer[it, pl.ds(units, rank)])

        @pl.loop(0, units // block)
        def _(b):
            first = pl.multiple_of(b * block, block)
            rows = pl.ds(first, block)
            q_copy(it, b, first, block).wait()
            old = w_ref[rows]
            new = old * (q_own[it, rows] + q_peer[it, rows]) / dot_packed(old, f_pack[...])
            w_ref[rows] = new
            wt[:rank, rows], wt[rank:, rows] = split(new.T)

    for store in h_store:
        store.wait()


def carry(w_ref, h_ref, w_out, h_out, sems):
    copies = [
        pltpu.make_async_copy(w_ref, w_out, sems.at[0]),
        pltpu.make_async_copy(h_ref, h_out, sems.at[1]),
    ]
    for copy in copies:
        copy.start()
    for copy in copies:
        copy.wait()


def shards(unit, abundance, unitig_factor, sample_factor):
    units, samples = abundance.shape
    rank = unitig_factor.shape[1]
    plan = Plan(unit, samples, rank)
    cols = plan.cols
    f32 = jnp.float32
    vmem = pl.BlockSpec(memory_space=pltpu.VMEM)
    blocks = units // 256 + 1
    flops = 4 * 3 * 2 * units * samples * rank
    hbm = pl.BlockSpec(memory_space=pl.ANY)
    results = (
        jax.ShapeDtypeStruct((units, rank), f32),
        jax.ShapeDtypeStruct((samples, rank), f32),
    )
    w_new, h_new = pl.pallas_call(
        functools.partial(kernel, plan),
        out_shape=results,
        in_specs=[hbm, vmem, hbm],
        out_specs=(vmem, hbm),
        scratch_shapes=[
            pltpu.VMEM((PARTS, units, cols), f32),
            pltpu.VMEM((PARTS, units, cols), BF),
            pltpu.VMEM((PARTS, units, cols), BF),
            pltpu.VMEM((2 * rank, units), BF),
            pltpu.VMEM((ITERS, plan.total, rank), f32),
            pltpu.VMEM((ITERS, plan.total, rank), f32),
            pltpu.VMEM((ITERS, plan.recv_rows, rank), f32),
            pltpu.VMEM((ITERS, units + rank, rank), f32),
            pltpu.VMEM((ITERS, units + rank, rank), f32),
            pltpu.VMEM((2 * rank, 2 * rank), BF),
            pltpu.VMEM((2 * rank, 2 * rank), BF),
            pltpu.VMEM((samples, rank), f32),
            pltpu.VMEM((cols, 2 * rank), BF),
            pltpu.SemaphoreType.DMA((PARTS,)),
            pltpu.SemaphoreType.DMA,
            pltpu.SemaphoreType.DMA((ITERS, plan.sems)),
            pltpu.SemaphoreType.DMA((ITERS, plan.sems)),
            pltpu.SemaphoreType.DMA((ITERS, plan.sems)),
            pltpu.SemaphoreType.DMA((ITERS, plan.sems)),
            pltpu.SemaphoreType.DMA((ITERS, blocks)),
            pltpu.SemaphoreType.DMA((ITERS, blocks)),
        ],
        compiler_params=pltpu.CompilerParams(
            collective_id=0, has_side_effects=True, vmem_limit_bytes=56 * 2**20
        ),
        cost_estimate=pl.CostEstimate(
            flops=flops, bytes_accessed=4 * units * samples, transcendentals=0
        ),
    )(abundance, unitig_factor, sample_factor)
    return pl.pallas_call(
        carry,
        out_shape=results,
        in_specs=[vmem, vmem],
        out_specs=(hbm, hbm),
        scratch_shapes=[pltpu.SemaphoreType.DMA((2,))],
    )(w_new, h_new)


def solution(mesh):
    return jax.shard_map(
        functools.partial(shards, mesh.shape["unit"]),
        mesh=mesh,
        in_specs=(P("unit", "samp"), P("unit", None), P("samp", None)),
        out_specs=(P("unit", None), P("samp", None)),
        check_vma=False,
    )
```

```python
import functools

import jax
import jax.numpy as jnp
from jax import lax
from jax.experimental import pallas as pl
from jax.experimental.pallas import tpu as pltpu
from jax.sharding import PartitionSpec as P

ITERS = 2
PARTS = 5
SHARES = (3, 3, 4, 3, 3)
ORDERS = ((2, 0, 1), (0, 1, 2), (1, 0, 2), (0, 1, 2), (1, 0, 2))
LEAD = 1
MESH = pl.DeviceIdType.MESH
BF = jnp.bfloat16


def chip_dims(unit):
    n = 1
    while 2 * n * n * n < unit:
        n += 1
    return (n, n, 2 * n) if 2 * n * n * n == unit else (1, 1, unit)


class Plan:
    def __init__(self, unit, samples, rank):
        self.unit = unit
        self.dims = chip_dims(unit)
        x, y, _ = self.dims
        self.strides = (1, x, x * y)
        self.orders = ORDERS
        self.cols = [samples // 16 * share for share in SHARES]
        self.first = [sum(self.cols[:p]) for p in range(PARTS)]
        granule = 8 * unit
        self.used = [self.cols[p] + (rank if p == LEAD else 0) for p in range(PARTS)]
        self.rows = [-(-used // granule) * granule for used in self.used]
        self.base = [sum(self.rows[:p]) for p in range(PARTS)]
        self.total = sum(self.rows)
        self.slot, self.sem = {}, {}
        rows = sems = 0
        for p in range(PARTS):
            size = self.rows[p]
            for t in range(3):
                n = self.dims[self.orders[p][t]]
                size //= n
                for k in range(1, n):
                    self.slot[p, t, k] = rows
                    self.sem[p, t, k] = sems
                    rows += size
                    sems += 1
        self.recv_rows, self.sems = max(rows, 8), max(sems, 1)


def split(value):
    high = value.astype(BF)
    return high, (value - high.astype(jnp.float32)).astype(BF)


def dot(left, right):
    return jnp.dot(left, right, preferred_element_type=jnp.float32)


def pack(square):
    high, low = split(square)
    return jnp.concatenate(
        [
            jnp.concatenate([high, low], axis=1),
            jnp.concatenate([high, jnp.zeros_like(high)], axis=1),
        ],
        axis=0,
    )


def dot_packed(left, packed):
    rank = left.shape[1]
    both = dot(jnp.concatenate(split(left), axis=1), packed)
    return both[:, :rank] + both[:, rank:]


def gram_of(turned, pair):
    rank = turned.shape[0] // 2
    four = dot(turned, pair)
    return four[:rank, :rank] + (
        four[rank:, :rank] + four[:rank, rank:] + four[rank:, rank:]
    )


EVENTS = (
    (1, 0), (2, 0), (3, 0), (0, 0), (4, 0), (1, 1), (2, 1), (0, 1), (3, 1), (4, 1),
    (1, 2), (2, 2), (0, 2), (3, 2), (4, 2), (1, 3), (0, 3), (2, 3), (0, 4), (3, 3),
    (4, 3), (1, 4), (2, 4), (3, 4), (4, 4), (1, 5), (2, 5), (0, 5), (3, 5), (4, 5),
)
LAST = EVENTS[-1][0]


def kernel(
    plan, a_hbm, w_in, h_in, w_ref, h_out,
    a_f32, a_high, a_low, wt, acc, gat, rsr, q_own, q_peer, g_pack, f_pack, h_ref,
    load_sem, h_sem, rs_send, rs_recv, ag_send, ag_recv, q_send, q_recv,
):
    units, rank = w_in.shape
    me = lax.axis_index("unit")
    core = lax.axis_index("samp")
    place = [lax.rem(me // plan.strides[d], plan.dims[d]) for d in range(3)]
    block = 256

    loads = [
        pltpu.make_async_copy(
            a_hbm.at[:, pl.ds(plan.first[p], plan.cols[p])],
            a_f32.at[:, pl.ds(plan.first[p], plan.cols[p])],
            load_sem.at[p],
        )
        for p in range(PARTS)
    ]
    for load in loads:
        load.start()
    h_load = pltpu.make_async_copy(h_in, h_ref, h_sem)
    h_load.start()

    def peer_of(d, k):
        other = lax.rem(place[d] + k, plan.dims[d])
        return other, me + (other - place[d]) * plan.strides[d]

    barrier = pltpu.get_barrier_semaphore()
    greeted = 1
    pl.semaphore_signal(barrier, inc=1, device_id={"samp": 1 - core}, device_id_type=MESH)
    for d in range(3):
        for k in range(1, plan.dims[d]):
            pl.semaphore_signal(
                barrier, inc=1, device_id={"unit": peer_of(d, k)[1]}, device_id_type=MESH
            )
            greeted += 1
    offs, sizes = [], []
    for p in range(PARTS):
        off, size = plan.base[p], plan.rows[p]
        offs.append([off])
        sizes.append([size])
        for t in range(3):
            d = plan.orders[p][t]
            size //= plan.dims[d]
            off = off + place[d] * size
            offs[p].append(off)
            sizes[p].append(size)

    def rows_at(off, size):
        return pl.ds(off if isinstance(off, int) else pl.multiple_of(off, 8), size)

    def rs_copies(it, p, t):
        d, size = plan.orders[p][t], sizes[p][t + 1]
        copies = []
        for k in range(1, plan.dims[d]):
            other, device = peer_of(d, k)
            sem = plan.sem[p, t, k]
            copies.append(pltpu.make_async_remote_copy(
                src_ref=acc.at[it, rows_at(offs[p][t] + other * size, size)],
                dst_ref=rsr.at[it, pl.ds(plan.slot[p, t, k], size)],
                send_sem=rs_send.at[it, sem],
                recv_sem=rs_recv.at[it, sem],
                device_id={"unit": device},
                device_id_type=MESH,
            ))
        return copies

    def ag_copies(it, p, t):
        d, size = plan.orders[p][t], sizes[p][t + 1]
        copies = []
        for k in range(1, plan.dims[d]):
            _, device = peer_of(d, k)
            sem = plan.sem[p, t, k]
            here = gat.at[it, rows_at(offs[p][t + 1], size)]
            copies.append(pltpu.make_async_remote_copy(
                src_ref=here,
                dst_ref=here,
                send_sem=ag_send.at[it, sem],
                recv_sem=ag_recv.at[it, sem],
                device_id={"unit": device},
                device_id_type=MESH,
            ))
        return copies

    def q_copy(it, b, start, size):
        return pltpu.make_async_remote_copy(
            src_ref=q_own.at[it, pl.ds(start, size)],
            dst_ref=q_peer.at[it, pl.ds(start, size)],
            send_sem=q_send.at[it, b],
            recv_sem=q_recv.at[it, b],
            device_id={"samp": 1 - core},
            device_id_type=MESH,
        )

    def start_all(copies):
        for copy in copies:
            copy.start()

    def products(it, p, sent):
        here = pl.ds(plan.first[p], plan.cols[p])
        if p == LEAD:
            acc[it, pl.ds(plan.base[p] + plan.cols[p], rank)] = gram_of(
                wt[...], jnp.concatenate(split(w_ref[...]), axis=1)
            )
        if plan.rows[p] > plan.used[p]:
            spare = plan.rows[p] - plan.used[p]
            acc[it, pl.ds(plan.base[p] + plan.used[p], spare)] = jnp.zeros(
                (spare, rank), jnp.float32
            )
        if it == 0:
            loads[p].wait()
            a_high[:, here], a_low[:, here] = split(a_f32[:, here])
        both = dot(wt[...], a_high[:, here])
        product = both[:rank] + (both[rank:] + dot(wt[:rank], a_low[:, here]))
        acc[it, pl.ds(plan.base[p], plan.cols[p])] = product.T
        if it == 0 and p == 0:
            pl.semaphore_wait(barrier, greeted)
        sent[p] = rs_copies(it, p, 0)
        start_all(sent[p])

    def advance(it, p, stage, sent):
        for copy in sent[p]:
            copy.wait()
        if stage < 3:
            size = sizes[p][stage + 1]
            mine = rows_at(offs[p][stage + 1], size)
            value = acc[it, mine]
            for k in range(1, plan.dims[plan.orders[p][stage]]):
                value = value + rsr[it, pl.ds(plan.slot[p, stage, k], size)]
            if stage < 2:
                acc[it, mine] = value
                sent[p] = rs_copies(it, p, stage + 1)
            else:
                gat[it, mine] = value
                sent[p] = ag_copies(it, p, 2)
            start_all(sent[p])
        elif stage < 5:
            sent[p] = ag_copies(it, p, 4 - stage)
            start_all(sent[p])

    def update_sample(it, p, h_store):
        if p == LEAD:
            g_pack[...] = pack(gat[it, pl.ds(plan.base[p] + plan.cols[p], rank)])
        here = pl.ds(plan.first[p], plan.cols[p])
        old = h_ref[here]
        new = old * gat[it, pl.ds(plan.base[p], plan.cols[p])] / dot_packed(old, g_pack[...])
        h_ref[here] = new
        if it == ITERS - 1:
            h_store[p].start()
        pair = jnp.concatenate(split(new), axis=1)
        turned = jnp.concatenate(split(new.T), axis=0)
        part_f = gram_of(turned, pair)
        tail = pl.ds(units, rank)
        q_own[it, tail] = part_f if p == LEAD else q_own[it, tail] + part_f
        crossing = []
        if p == LAST:
            crossing.append(q_copy(it, 0, units, rank))
            crossing[0].start()
        for b in range(units // block):
            rows = pl.ds(b * block, block)
            both = dot(a_high[rows, here], pair)
            value = both[:, :rank] + (both[:, rank:] + dot(a_low[rows, here], pair[:, :rank]))
            q_own[it, rows] = value if p == LEAD else q_own[it, rows] + value
            if p == LAST:
                crossing.append(q_copy(it, b + 1, b * block, block))
                crossing[-1].start()
        return crossing

    w_ref[...] = w_in[...]
    turned = w_in[...].T
    wt[:rank], wt[rank:] = split(turned)
    h_store = [
        pltpu.make_async_copy(
            h_ref.at[pl.ds(plan.first[p], plan.cols[p])],
            h_out.at[pl.ds(plan.first[p], plan.cols[p])],
            load_sem.at[p],
        )
        for p in range(PARTS)
    ]

    for it in range(ITERS):
        sent = {}
        for p in range(PARTS):
            products(it, p, sent)
        if it == 0:
            h_load.wait()
        crossing = []
        for p, stage in EVENTS:
            advance(it, p, stage, sent)
            if stage == 5:
                crossing = update_sample(it, p, h_store)

        crossing[0].wait()
        f_pack[...] = pack(q_own[it, pl.ds(units, rank)] + q_peer[it, pl.ds(units, rank)])
        for b in range(units // block):
            rows = pl.ds(b * block, block)
            crossing[b + 1].wait()
            old = w_ref[rows]
            new = old * (q_own[it, rows] + q_peer[it, rows]) / dot_packed(old, f_pack[...])
            w_ref[rows] = new
            if it < ITERS - 1:
                wt[:rank, rows], wt[rank:, rows] = split(new.T)
    for store in h_store:
        store.wait()


def carry(w_ref, h_ref, w_out, h_out, sems):
    copies = [
        pltpu.make_async_copy(w_ref, w_out, sems.at[0]),
        pltpu.make_async_copy(h_ref, h_out, sems.at[1]),
    ]
    for copy in copies:
        copy.start()
    for copy in copies:
        copy.wait()


def shards(unit, abundance, unitig_factor, sample_factor):
    units, samples = abundance.shape
    rank = unitig_factor.shape[1]
    plan = Plan(unit, samples, rank)
    f32 = jnp.float32
    vmem = pl.BlockSpec(memory_space=pltpu.VMEM)
    blocks = units // 256 + 1
    flops = 4 * 3 * 2 * units * samples * rank
    hbm = pl.BlockSpec(memory_space=pl.ANY)
    results = (
        jax.ShapeDtypeStruct((units, rank), f32),
        jax.ShapeDtypeStruct((samples, rank), f32),
    )
    w_new, h_new = pl.pallas_call(
        functools.partial(kernel, plan),
        out_shape=results,
        in_specs=[hbm, vmem, hbm],
        out_specs=(vmem, hbm),
        scratch_shapes=[
            pltpu.VMEM((units, samples), f32),
            pltpu.VMEM((units, samples), BF),
            pltpu.VMEM((units, samples), BF),
            pltpu.VMEM((2 * rank, units), BF),
            pltpu.VMEM((ITERS, plan.total, rank), f32),
            pltpu.VMEM((ITERS, plan.total, rank), f32),
            pltpu.VMEM((ITERS, plan.recv_rows, rank), f32),
            pltpu.VMEM((ITERS, units + rank, rank), f32),
            pltpu.VMEM((ITERS, units + rank, rank), f32),
            pltpu.VMEM((2 * rank, 2 * rank), BF),
            pltpu.VMEM((2 * rank, 2 * rank), BF),
            pltpu.VMEM((samples, rank), f32),
            pltpu.SemaphoreType.DMA((PARTS,)),
            pltpu.SemaphoreType.DMA,
            pltpu.SemaphoreType.DMA((ITERS, plan.sems)),
            pltpu.SemaphoreType.DMA((ITERS, plan.sems)),
            pltpu.SemaphoreType.DMA((ITERS, plan.sems)),
            pltpu.SemaphoreType.DMA((ITERS, plan.sems)),
            pltpu.SemaphoreType.DMA((ITERS, blocks)),
            pltpu.SemaphoreType.DMA((ITERS, blocks)),
        ],
        compiler_params=pltpu.CompilerParams(
            collective_id=0, has_side_effects=True, vmem_limit_bytes=56 * 2**20
        ),
        cost_estimate=pl.CostEstimate(
            flops=flops, bytes_accessed=4 * units * samples, transcendentals=0
        ),
    )(abundance, unitig_factor, sample_factor)
    return pl.pallas_call(
        carry,
        out_shape=results,
        in_specs=[vmem, vmem],
        out_specs=(hbm, hbm),
        scratch_shapes=[pltpu.SemaphoreType.DMA((2,))],
    )(w_new, h_new)


def solution(mesh):
    return jax.shard_map(
        functools.partial(shards, mesh.shape["unit"]),
        mesh=mesh,
        in_specs=(P("unit", "samp"), P("unit", None), P("samp", None)),
        out_specs=(P("unit", None), P("samp", None)),
        check_vma=False,
    )
```

```python
import functools

import jax
import jax.numpy as jnp
from jax import lax
from jax.experimental import pallas as pl
from jax.experimental.pallas import tpu as pltpu
from jax.sharding import PartitionSpec as P

ITERS = 2
PARTS = 5
SHARES = (2, 4, 4, 4, 2)
ORDERS = ((2, 0, 1), (0, 1, 2), (1, 0, 2), (1, 0, 2), (0, 1, 2))
LEAD = 1
MESH = pl.DeviceIdType.MESH
BF = jnp.bfloat16


def chip_dims(unit):
    n = 1
    while 2 * n * n * n < unit:
        n += 1
    return (n, n, 2 * n) if 2 * n * n * n == unit else (1, 1, unit)


class Plan:
    def __init__(self, unit, samples, rank):
        self.unit = unit
        self.dims = chip_dims(unit)
        x, y, _ = self.dims
        self.strides = (1, x, x * y)
        self.orders = ORDERS
        self.cols = [samples // 16 * share for share in SHARES]
        self.first = [sum(self.cols[:p]) for p in range(PARTS)]
        granule = 8 * unit
        self.used = [self.cols[p] + (rank if p == LEAD else 0) for p in range(PARTS)]
        self.rows = [-(-used // granule) * granule for used in self.used]
        self.base = [sum(self.rows[:p]) for p in range(PARTS)]
        self.total = sum(self.rows)
        self.slot, self.sem = {}, {}
        rows = sems = 0
        for p in range(PARTS):
            size = self.rows[p]
            for t in range(3):
                n = self.dims[self.orders[p][t]]
                size //= n
                for k in range(1, n):
                    self.slot[p, t, k] = rows
                    self.sem[p, t, k] = sems
                    rows += size
                    sems += 1
        self.recv_rows, self.sems = max(rows, 8), max(sems, 1)


def split(value):
    high = value.astype(BF)
    return high, (value - high.astype(jnp.float32)).astype(BF)


def dot(left, right):
    return jnp.dot(left, right, preferred_element_type=jnp.float32)


def pack(square):
    high, low = split(square)
    return jnp.concatenate(
        [
            jnp.concatenate([high, low], axis=1),
            jnp.concatenate([high, jnp.zeros_like(high)], axis=1),
        ],
        axis=0,
    )


def dot_packed(left, packed):
    rank = left.shape[1]
    both = dot(jnp.concatenate(split(left), axis=1), packed)
    return both[:, :rank] + both[:, rank:]


def gram_of(turned, pair):
    rank = turned.shape[0] // 2
    four = dot(turned, pair)
    return four[:rank, :rank] + (
        four[rank:, :rank] + four[:rank, rank:] + four[rank:, rank:]
    )


EVENTS = (
    (1, 0), (0, 0), (2, 0), (4, 0), (3, 0), (1, 1), (2, 1), (0, 1), (4, 1), (3, 1),
    (1, 2), (2, 2), (0, 2), (4, 2), (3, 2), (1, 3), (0, 3), (2, 3), (0, 4), (4, 3),
    (3, 3), (1, 4), (2, 4), (4, 4), (3, 4), (1, 5), (2, 5), (0, 5), (4, 5), (3, 5),
)
LAST = EVENTS[-1][0]


def kernel(
    plan, a_hbm, w_in, h_in, w_ref, h_out,
    a_f32, a_high, a_low, wt, acc, gat, rsr, q_own, q_peer, g_pack, f_pack, h_ref,
    load_sem, h_sem, rs_send, rs_recv, ag_send, ag_recv, q_send, q_recv,
):
    units, rank = w_in.shape
    me = lax.axis_index("unit")
    core = lax.axis_index("samp")
    place = [lax.rem(me // plan.strides[d], plan.dims[d]) for d in range(3)]
    block = 256

    loads = [
        pltpu.make_async_copy(
            a_hbm.at[:, pl.ds(plan.first[p], plan.cols[p])],
            a_f32.at[:, pl.ds(plan.first[p], plan.cols[p])],
            load_sem.at[p],
        )
        for p in range(PARTS)
    ]
    for p in (0, 1, 2, 4, 3):
        loads[p].start()
    h_load = pltpu.make_async_copy(h_in, h_ref, h_sem)
    h_load.start()

    def peer_of(d, k):
        other = lax.rem(place[d] + k, plan.dims[d])
        return other, me + (other - place[d]) * plan.strides[d]

    barrier = pltpu.get_barrier_semaphore()
    greeted = 1
    pl.semaphore_signal(barrier, inc=1, device_id={"samp": 1 - core}, device_id_type=MESH)
    for d in range(3):
        for k in range(1, plan.dims[d]):
            pl.semaphore_signal(
                barrier, inc=1, device_id={"unit": peer_of(d, k)[1]}, device_id_type=MESH
            )
            greeted += 1
    offs, sizes = [], []
    for p in range(PARTS):
        off, size = plan.base[p], plan.rows[p]
        offs.append([off])
        sizes.append([size])
        for t in range(3):
            d = plan.orders[p][t]
            size //= plan.dims[d]
            off = off + place[d] * size
            offs[p].append(off)
            sizes[p].append(size)

    def rows_at(off, size):
        return pl.ds(off if isinstance(off, int) else pl.multiple_of(off, 8), size)

    def rs_copies(it, p, t):
        d, size = plan.orders[p][t], sizes[p][t + 1]
        copies = []
        for k in range(1, plan.dims[d]):
            other, device = peer_of(d, k)
            sem = plan.sem[p, t, k]
            copies.append(pltpu.make_async_remote_copy(
                src_ref=acc.at[it, rows_at(offs[p][t] + other * size, size)],
                dst_ref=rsr.at[it, pl.ds(plan.slot[p, t, k], size)],
                send_sem=rs_send.at[it, sem],
                recv_sem=rs_recv.at[it, sem],
                device_id={"unit": device},
                device_id_type=MESH,
            ))
        return copies

    def ag_copies(it, p, t):
        d, size = plan.orders[p][t], sizes[p][t + 1]
        copies = []
        for k in range(1, plan.dims[d]):
            _, device = peer_of(d, k)
            sem = plan.sem[p, t, k]
            here = gat.at[it, rows_at(offs[p][t + 1], size)]
            copies.append(pltpu.make_async_remote_copy(
                src_ref=here,
                dst_ref=here,
                send_sem=ag_send.at[it, sem],
                recv_sem=ag_recv.at[it, sem],
                device_id={"unit": device},
                device_id_type=MESH,
            ))
        return copies

    def q_copy(it, b, start, size):
        return pltpu.make_async_remote_copy(
            src_ref=q_own.at[it, pl.ds(start, size)],
            dst_ref=q_peer.at[it, pl.ds(start, size)],
            send_sem=q_send.at[it, b],
            recv_sem=q_recv.at[it, b],
            device_id={"samp": 1 - core},
            device_id_type=MESH,
        )

    def start_all(copies):
        for copy in copies:
            copy.start()

    def products(it, p, sent):
        here = pl.ds(plan.first[p], plan.cols[p])
        if p == LEAD:
            acc[it, pl.ds(plan.base[p] + plan.cols[p], rank)] = gram_of(
                wt[...], jnp.concatenate(split(w_ref[...]), axis=1)
            )
        if plan.rows[p] > plan.used[p]:
            spare = plan.rows[p] - plan.used[p]
            acc[it, pl.ds(plan.base[p] + plan.used[p], spare)] = jnp.zeros(
                (spare, rank), jnp.float32
            )
        if it == 0:
            loads[p].wait()
            a_high[:, here], a_low[:, here] = split(a_f32[:, here])
        both = dot(wt[...], a_high[:, here])
        product = both[:rank] + (both[rank:] + dot(wt[:rank], a_low[:, here]))
        acc[it, pl.ds(plan.base[p], plan.cols[p])] = product.T
        if it == 0 and p == 0:
            pl.semaphore_wait(barrier, greeted)
        sent[p] = rs_copies(it, p, 0)
        start_all(sent[p])

    def advance(it, p, stage, sent):
        for copy in sent[p]:
            copy.wait()
        if stage < 3:
            size = sizes[p][stage + 1]
            mine = rows_at(offs[p][stage + 1], size)
            value = acc[it, mine]
            for k in range(1, plan.dims[plan.orders[p][stage]]):
                value = value + rsr[it, pl.ds(plan.slot[p, stage, k], size)]
            if stage < 2:
                acc[it, mine] = value
                sent[p] = rs_copies(it, p, stage + 1)
            else:
                gat[it, mine] = value
                sent[p] = ag_copies(it, p, 2)
            start_all(sent[p])
        elif stage < 5:
            sent[p] = ag_copies(it, p, 4 - stage)
            start_all(sent[p])

    def update_sample(it, p, h_store):
        if p == LEAD:
            g_pack[...] = pack(gat[it, pl.ds(plan.base[p] + plan.cols[p], rank)])
        here = pl.ds(plan.first[p], plan.cols[p])
        old = h_ref[here]
        new = old * gat[it, pl.ds(plan.base[p], plan.cols[p])] / dot_packed(old, g_pack[...])
        h_ref[here] = new
        if it == ITERS - 1:
            h_store[p].start()
        pair = jnp.concatenate(split(new), axis=1)
        turned = jnp.concatenate(split(new.T), axis=0)
        part_f = gram_of(turned, pair)
        tail = pl.ds(units, rank)
        q_own[it, tail] = part_f if p == LEAD else q_own[it, tail] + part_f
        crossing = []
        if p == LAST:
            crossing.append(q_copy(it, 0, units, rank))
            crossing[0].start()
        for b in range(units // block):
            rows = pl.ds(b * block, block)
            both = dot(a_high[rows, here], pair)
            value = both[:, :rank] + (both[:, rank:] + dot(a_low[rows, here], pair[:, :rank]))
            q_own[it, rows] = value if p == LEAD else q_own[it, rows] + value
            if p == LAST:
                crossing.append(q_copy(it, b + 1, b * block, block))
                crossing[-1].start()
        return crossing

    w_ref[...] = w_in[...]
    turned = w_in[...].T
    wt[:rank], wt[rank:] = split(turned)
    h_store = [
        pltpu.make_async_copy(
            h_ref.at[pl.ds(plan.first[p], plan.cols[p])],
            h_out.at[pl.ds(plan.first[p], plan.cols[p])],
            load_sem.at[p],
        )
        for p in range(PARTS)
    ]

    for it in range(ITERS):
        sent = {}
        for p in (0, 1, 2, 4, 3):
            products(it, p, sent)
        if it == 0:
            h_load.wait()
        crossing = []
        for p, stage in EVENTS:
            advance(it, p, stage, sent)
            if stage == 5:
                crossing = update_sample(it, p, h_store)

        crossing[0].wait()
        f_pack[...] = pack(q_own[it, pl.ds(units, rank)] + q_peer[it, pl.ds(units, rank)])
        for b in range(units // block):
            rows = pl.ds(b * block, block)
            crossing[b + 1].wait()
            old = w_ref[rows]
            new = old * (q_own[it, rows] + q_peer[it, rows]) / dot_packed(old, f_pack[...])
            w_ref[rows] = new
            if it < ITERS - 1:
                wt[:rank, rows], wt[rank:, rows] = split(new.T)
    for store in h_store:
        store.wait()


def carry(w_ref, h_ref, w_out, h_out, sems):
    copies = [
        pltpu.make_async_copy(w_ref, w_out, sems.at[0]),
        pltpu.make_async_copy(h_ref, h_out, sems.at[1]),
    ]
    for copy in copies:
        copy.start()
    for copy in copies:
        copy.wait()


def shards(unit, abundance, unitig_factor, sample_factor):
    units, samples = abundance.shape
    rank = unitig_factor.shape[1]
    plan = Plan(unit, samples, rank)
    f32 = jnp.float32
    vmem = pl.BlockSpec(memory_space=pltpu.VMEM)
    blocks = units // 256 + 1
    flops = 4 * 3 * 2 * units * samples * rank
    hbm = pl.BlockSpec(memory_space=pl.ANY)
    results = (
        jax.ShapeDtypeStruct((units, rank), f32),
        jax.ShapeDtypeStruct((samples, rank), f32),
    )
    w_new, h_new = pl.pallas_call(
        functools.partial(kernel, plan),
        out_shape=results,
        in_specs=[hbm, vmem, hbm],
        out_specs=(vmem, hbm),
        scratch_shapes=[
            pltpu.VMEM((units, samples), f32),
            pltpu.VMEM((units, samples), BF),
            pltpu.VMEM((units, samples), BF),
            pltpu.VMEM((2 * rank, units), BF),
            pltpu.VMEM((ITERS, plan.total, rank), f32),
            pltpu.VMEM((ITERS, plan.total, rank), f32),
            pltpu.VMEM((ITERS, plan.recv_rows, rank), f32),
            pltpu.VMEM((ITERS, units + rank, rank), f32),
            pltpu.VMEM((ITERS, units + rank, rank), f32),
            pltpu.VMEM((2 * rank, 2 * rank), BF),
            pltpu.VMEM((2 * rank, 2 * rank), BF),
            pltpu.VMEM((samples, rank), f32),
            pltpu.SemaphoreType.DMA((PARTS,)),
            pltpu.SemaphoreType.DMA,
            pltpu.SemaphoreType.DMA((ITERS, plan.sems)),
            pltpu.SemaphoreType.DMA((ITERS, plan.sems)),
            pltpu.SemaphoreType.DMA((ITERS, plan.sems)),
            pltpu.SemaphoreType.DMA((ITERS, plan.sems)),
            pltpu.SemaphoreType.DMA((ITERS, blocks)),
            pltpu.SemaphoreType.DMA((ITERS, blocks)),
        ],
        compiler_params=pltpu.CompilerParams(
            collective_id=0, has_side_effects=True, vmem_limit_bytes=56 * 2**20
        ),
        cost_estimate=pl.CostEstimate(
            flops=flops, bytes_accessed=4 * units * samples, transcendentals=0
        ),
    )(abundance, unitig_factor, sample_factor)
    return pl.pallas_call(
        carry,
        out_shape=results,
        in_specs=[vmem, vmem],
        out_specs=(hbm, hbm),
        scratch_shapes=[pltpu.SemaphoreType.DMA((2,))],
    )(w_new, h_new)


def solution(mesh):
    return jax.shard_map(
        functools.partial(shards, mesh.shape["unit"]),
        mesh=mesh,
        in_specs=(P("unit", "samp"), P("unit", None), P("samp", None)),
        out_specs=(P("unit", None), P("samp", None)),
        check_vma=False,
    )
```

```python
import functools

import jax
import jax.numpy as jnp
from jax import lax
from jax.experimental import pallas as pl
from jax.experimental.pallas import tpu as pltpu
from jax.sharding import PartitionSpec as P

ITERS = 2
PARTS = 4
SHARES = (4, 4, 4, 4)
ORDERS = ((2, 0, 1), (0, 1, 2), (1, 0, 2), (1, 0, 2))
LEAD = 1
MESH = pl.DeviceIdType.MESH
BF = jnp.bfloat16


def chip_dims(unit):
    n = 1
    while 2 * n * n * n < unit:
        n += 1
    return (n, n, 2 * n) if 2 * n * n * n == unit else (1, 1, unit)


class Plan:
    def __init__(self, unit, samples, rank):
        self.unit = unit
        self.dims = chip_dims(unit)
        x, y, _ = self.dims
        self.strides = (1, x, x * y)
        self.orders = ORDERS
        self.cols = [samples // 16 * share for share in SHARES]
        self.first = [sum(self.cols[:p]) for p in range(PARTS)]
        granule = 8 * unit
        self.used = [self.cols[p] + (rank if p == LEAD else 0) for p in range(PARTS)]
        self.rows = [-(-used // granule) * granule for used in self.used]
        self.base = [sum(self.rows[:p]) for p in range(PARTS)]
        self.total = sum(self.rows)
        self.slot, self.sem = {}, {}
        rows = sems = 0
        for p in range(PARTS):
            size = self.rows[p]
            for t in range(3):
                n = self.dims[self.orders[p][t]]
                size //= n
                for k in range(1, n):
                    self.slot[p, t, k] = rows
                    self.sem[p, t, k] = sems
                    rows += size
                    sems += 1
        self.recv_rows, self.sems = max(rows, 8), max(sems, 1)


def split(value):
    high = value.astype(BF)
    return high, (value - high.astype(jnp.float32)).astype(BF)


def dot(left, right):
    return jnp.dot(left, right, preferred_element_type=jnp.float32)


def pack(square):
    high, low = split(square)
    return jnp.concatenate(
        [
            jnp.concatenate([high, low], axis=1),
            jnp.concatenate([high, jnp.zeros_like(high)], axis=1),
        ],
        axis=0,
    )


def dot_packed(left, packed):
    rank = left.shape[1]
    both = dot(jnp.concatenate(split(left), axis=1), packed)
    return both[:, :rank] + both[:, rank:]


def gram_of(turned, pair):
    rank = turned.shape[0] // 2
    four = dot(turned, pair)
    return four[:rank, :rank] + (
        four[rank:, :rank] + four[:rank, rank:] + four[rank:, rank:]
    )


EVENTS = (
    (1, 0), (2, 0), (0, 0), (3, 0), (1, 1), (2, 1), (0, 1), (3, 1),
    (1, 2), (2, 2), (0, 2), (3, 2), (1, 3), (0, 3), (2, 3), (0, 4),
    (3, 3), (1, 4), (2, 4), (3, 4), (1, 5), (2, 5), (0, 5), (3, 5),
)
LAST = EVENTS[-1][0]


def kernel(
    plan, a_hbm, w_in, h_in, w_ref, h_out,
    a_f32, a_high, a_low, wt, acc, gat, rsr, q_own, q_peer, g_pack, f_pack, h_ref,
    load_sem, h_sem, rs_send, rs_recv, ag_send, ag_recv, q_send, q_recv,
):
    units, rank = w_in.shape
    me = lax.axis_index("unit")
    core = lax.axis_index("samp")
    place = [lax.rem(me // plan.strides[d], plan.dims[d]) for d in range(3)]
    block = 256

    loads = [
        pltpu.make_async_copy(
            a_hbm.at[:, pl.ds(plan.first[p], plan.cols[p])],
            a_f32.at[:, pl.ds(plan.first[p], plan.cols[p])],
            load_sem.at[p],
        )
        for p in range(PARTS)
    ]
    for load in loads:
        load.start()
    h_load = pltpu.make_async_copy(h_in, h_ref, h_sem)
    h_load.start()

    def peer_of(d, k):
        other = lax.rem(place[d] + k, plan.dims[d])
        return other, me + (other - place[d]) * plan.strides[d]

    barrier = pltpu.get_barrier_semaphore()
    greeted = 1
    pl.semaphore_signal(barrier, inc=1, device_id={"samp": 1 - core}, device_id_type=MESH)
    for d in range(3):
        for k in range(1, plan.dims[d]):
            pl.semaphore_signal(
                barrier, inc=1, device_id={"unit": peer_of(d, k)[1]}, device_id_type=MESH
            )
            greeted += 1
    offs, sizes = [], []
    for p in range(PARTS):
        off, size = plan.base[p], plan.rows[p]
        offs.append([off])
        sizes.append([size])
        for t in range(3):
            d = plan.orders[p][t]
            size //= plan.dims[d]
            off = off + place[d] * size
            offs[p].append(off)
            sizes[p].append(size)

    def rows_at(off, size):
        return pl.ds(off if isinstance(off, int) else pl.multiple_of(off, 8), size)

    def rs_copies(it, p, t):
        d, size = plan.orders[p][t], sizes[p][t + 1]
        copies = []
        for k in range(1, plan.dims[d]):
            other, device = peer_of(d, k)
            sem = plan.sem[p, t, k]
            copies.append(pltpu.make_async_remote_copy(
                src_ref=acc.at[it, rows_at(offs[p][t] + other * size, size)],
                dst_ref=rsr.at[it, pl.ds(plan.slot[p, t, k], size)],
                send_sem=rs_send.at[it, sem],
                recv_sem=rs_recv.at[it, sem],
                device_id={"unit": device},
                device_id_type=MESH,
            ))
        return copies

    def ag_copies(it, p, t):
        d, size = plan.orders[p][t], sizes[p][t + 1]
        copies = []
        for k in range(1, plan.dims[d]):
            _, device = peer_of(d, k)
            sem = plan.sem[p, t, k]
            here = gat.at[it, rows_at(offs[p][t + 1], size)]
            copies.append(pltpu.make_async_remote_copy(
                src_ref=here,
                dst_ref=here,
                send_sem=ag_send.at[it, sem],
                recv_sem=ag_recv.at[it, sem],
                device_id={"unit": device},
                device_id_type=MESH,
            ))
        return copies

    def q_copy(it, b, start, size):
        return pltpu.make_async_remote_copy(
            src_ref=q_own.at[it, pl.ds(start, size)],
            dst_ref=q_peer.at[it, pl.ds(start, size)],
            send_sem=q_send.at[it, b],
            recv_sem=q_recv.at[it, b],
            device_id={"samp": 1 - core},
            device_id_type=MESH,
        )

    def start_all(copies):
        for copy in copies:
            copy.start()

    def products(it, p, sent):
        here = pl.ds(plan.first[p], plan.cols[p])
        if p == LEAD:
            acc[it, pl.ds(plan.base[p] + plan.cols[p], rank)] = gram_of(
                wt[...], jnp.concatenate(split(w_ref[...]), axis=1)
            )
        if plan.rows[p] > plan.used[p]:
            spare = plan.rows[p] - plan.used[p]
            acc[it, pl.ds(plan.base[p] + plan.used[p], spare)] = jnp.zeros(
                (spare, rank), jnp.float32
            )
        if it == 0:
            loads[p].wait()
            a_high[:, here], a_low[:, here] = split(a_f32[:, here])
        both = dot(wt[...], a_high[:, here])
        product = both[:rank] + (both[rank:] + dot(wt[:rank], a_low[:, here]))
        acc[it, pl.ds(plan.base[p], plan.cols[p])] = product.T
        if it == 0 and p == 0:
            pl.semaphore_wait(barrier, greeted)
        sent[p] = rs_copies(it, p, 0)
        start_all(sent[p])

    def advance(it, p, stage, sent):
        for copy in sent[p]:
            copy.wait()
        if stage < 3:
            size = sizes[p][stage + 1]
            mine = rows_at(offs[p][stage + 1], size)
            value = acc[it, mine]
            for k in range(1, plan.dims[plan.orders[p][stage]]):
                value = value + rsr[it, pl.ds(plan.slot[p, stage, k], size)]
            if stage < 2:
                acc[it, mine] = value
                sent[p] = rs_copies(it, p, stage + 1)
            else:
                gat[it, mine] = value
                sent[p] = ag_copies(it, p, 2)
            start_all(sent[p])
        elif stage < 5:
            sent[p] = ag_copies(it, p, 4 - stage)
            start_all(sent[p])

    def update_sample(it, p, h_store):
        if p == LEAD:
            g_pack[...] = pack(gat[it, pl.ds(plan.base[p] + plan.cols[p], rank)])
        here = pl.ds(plan.first[p], plan.cols[p])
        old = h_ref[here]
        new = old * gat[it, pl.ds(plan.base[p], plan.cols[p])] / dot_packed(old, g_pack[...])
        h_ref[here] = new
        if it == ITERS - 1:
            h_store[p].start()
        pair = jnp.concatenate(split(new), axis=1)
        turned = jnp.concatenate(split(new.T), axis=0)
        part_f = gram_of(turned, pair)
        tail = pl.ds(units, rank)
        q_own[it, tail] = part_f if p == LEAD else q_own[it, tail] + part_f
        crossing = []
        if p == LAST:
            crossing.append(q_copy(it, 0, units, rank))
            crossing[0].start()
        for b in range(units // block):
            rows = pl.ds(b * block, block)
            both = dot(a_high[rows, here], pair)
            value = both[:, :rank] + (both[:, rank:] + dot(a_low[rows, here], pair[:, :rank]))
            q_own[it, rows] = value if p == LEAD else q_own[it, rows] + value
            if p == LAST:
                crossing.append(q_copy(it, b + 1, b * block, block))
                crossing[-1].start()
        return crossing

    w_ref[...] = w_in[...]
    turned = w_in[...].T
    wt[:rank], wt[rank:] = split(turned)
    h_store = [
        pltpu.make_async_copy(
            h_ref.at[pl.ds(plan.first[p], plan.cols[p])],
            h_out.at[pl.ds(plan.first[p], plan.cols[p])],
            load_sem.at[p],
        )
        for p in range(PARTS)
    ]

    for it in range(ITERS):
        sent = {}
        for p in range(PARTS):
            products(it, p, sent)
        if it == 0:
            h_load.wait()
        crossing = []
        for p, stage in EVENTS:
            advance(it, p, stage, sent)
            if stage == 5:
                crossing = update_sample(it, p, h_store)

        crossing[0].wait()
        f_pack[...] = pack(q_own[it, pl.ds(units, rank)] + q_peer[it, pl.ds(units, rank)])
        for b in range(units // block):
            rows = pl.ds(b * block, block)
            crossing[b + 1].wait()
            old = w_ref[rows]
            new = old * (q_own[it, rows] + q_peer[it, rows]) / dot_packed(old, f_pack[...])
            w_ref[rows] = new
            if it < ITERS - 1:
                wt[:rank, rows], wt[rank:, rows] = split(new.T)
    for store in h_store:
        store.wait()


def carry(w_ref, h_ref, w_out, h_out, sems):
    copies = [
        pltpu.make_async_copy(w_ref, w_out, sems.at[0]),
        pltpu.make_async_copy(h_ref, h_out, sems.at[1]),
    ]
    for copy in copies:
        copy.start()
    for copy in copies:
        copy.wait()


def shards(unit, abundance, unitig_factor, sample_factor):
    units, samples = abundance.shape
    rank = unitig_factor.shape[1]
    plan = Plan(unit, samples, rank)
    f32 = jnp.float32
    vmem = pl.BlockSpec(memory_space=pltpu.VMEM)
    blocks = units // 256 + 1
    flops = 4 * 3 * 2 * units * samples * rank
    hbm = pl.BlockSpec(memory_space=pl.ANY)
    results = (
        jax.ShapeDtypeStruct((units, rank), f32),
        jax.ShapeDtypeStruct((samples, rank), f32),
    )
    w_new, h_new = pl.pallas_call(
        functools.partial(kernel, plan),
        out_shape=results,
        in_specs=[hbm, vmem, hbm],
        out_specs=(vmem, hbm),
        scratch_shapes=[
            pltpu.VMEM((units, samples), f32),
            pltpu.VMEM((units, samples), BF),
            pltpu.VMEM((units, samples), BF),
            pltpu.VMEM((2 * rank, units), BF),
            pltpu.VMEM((ITERS, plan.total, rank), f32),
            pltpu.VMEM((ITERS, plan.total, rank), f32),
            pltpu.VMEM((ITERS, plan.recv_rows, rank), f32),
            pltpu.VMEM((ITERS, units + rank, rank), f32),
            pltpu.VMEM((ITERS, units + rank, rank), f32),
            pltpu.VMEM((2 * rank, 2 * rank), BF),
            pltpu.VMEM((2 * rank, 2 * rank), BF),
            pltpu.VMEM((samples, rank), f32),
            pltpu.SemaphoreType.DMA((PARTS,)),
            pltpu.SemaphoreType.DMA,
            pltpu.SemaphoreType.DMA((ITERS, plan.sems)),
            pltpu.SemaphoreType.DMA((ITERS, plan.sems)),
            pltpu.SemaphoreType.DMA((ITERS, plan.sems)),
            pltpu.SemaphoreType.DMA((ITERS, plan.sems)),
            pltpu.SemaphoreType.DMA((ITERS, blocks)),
            pltpu.SemaphoreType.DMA((ITERS, blocks)),
        ],
        compiler_params=pltpu.CompilerParams(
            collective_id=0, has_side_effects=True, vmem_limit_bytes=56 * 2**20
        ),
        cost_estimate=pl.CostEstimate(
            flops=flops, bytes_accessed=4 * units * samples, transcendentals=0
        ),
    )(abundance, unitig_factor, sample_factor)
    return pl.pallas_call(
        carry,
        out_shape=results,
        in_specs=[vmem, vmem],
        out_specs=(hbm, hbm),
        scratch_shapes=[pltpu.SemaphoreType.DMA((2,))],
    )(w_new, h_new)


def solution(mesh):
    return jax.shard_map(
        functools.partial(shards, mesh.shape["unit"]),
        mesh=mesh,
        in_specs=(P("unit", "samp"), P("unit", None), P("samp", None)),
        out_specs=(P("unit", None), P("samp", None)),
        check_vma=False,
    )
```
